32 devices in a mesh: groups: 2 (over x), slab: 2 (over core), tm: 8 (over z, y).
Axes of the slice: x: 2, y: 2, z: 4, core: 2. Of those that a mesh axis runs over, the one named last changes fastest.
Arguments:
- demand: int32 [8, 256], P('groups', ('slab', 'tm')), parts along dimension 0, may hold values from 0 to 20
- lead_offset: int32 [8, 256], P('groups', ('slab', 'tm')), parts along dimension 0, may hold values from 0 to 7
- review: int32 [8, 256], P('groups', ('slab', 'tm')), parts along dimension 0, may hold values 0 or 1
- scenario_id: int32 [8], P('groups'), parts along dimension 0, may hold values from 0 to 15
- initial_state: float32 [8, 128], P('groups'), parts along dimension 0, may hold values from -2.5 to 2.5
- guess: float32 [8, 256, 128], P('groups', ('slab', 'tm')), parts along dimension 0, may hold values from -0.9 to 0.9
- input_weight: float32 [16, 384], replicated, may hold values from -1.5 to 1.5
- scenario_table: float32 [16, 384], replicated, may hold values from -3 to 3
- recur_weight: float32 [128, 384], replicated, may hold values from -0.5 to 0.5
- update_bias: float32 [128], replicated, may hold values from -1.5 to 10
- review_depth: float32 [128], replicated, may hold values from 0.8 to 0.95
Outputs:
- trajectory: float32 [8, 256, 128], P('groups', ('slab', 'tm')), parts along dimension 0
The draws below stay inside these ranges and needn't reach their ends.
There are 2 independent parts, one for each index of `groups`. The reference program is written for one: setup_inputs(seed, part) draws one part's arguments, and reference() takes and returns one part's arrays. A program takes and returns all parts, laid end to end along the dimension named above; an argument that names none is the same for every part. Nothing has to cross between parts.
All inputs are finite; a program needn't handle non-finite values. No bound on the sum of `review` on one device may be relied on, other than what follows from the above.
Results may differ from the reference program's by a relative error of at most 0.0003.
Values sent between devices are 32-bit elements; how exact they have to be, the bound alone decides.
A program may use at most 128 MiB of HBM per device.

```python
import jax
import jax.numpy as jnp
from jax import lax

H = 128
LEAD = 8
S = 4
NSCEN = 16
NEWTON = 2
TOTAL = 256


def draw_update_bias(key, part):
    key = jax.random.fold_in(key, 7)
    key_pick, key_fast, key_slow = jax.random.split(key, 3)
    share = 0.5
    pick = jax.random.uniform(key_pick, (H,), dtype=jnp.float32) < share
    fast = jax.random.uniform(key_fast, (H,), dtype=jnp.float32, minval=-1.5, maxval=3.5)
    slow = jax.random.uniform(key_slow, (H,), dtype=jnp.float32, minval=8.5, maxval=10.0)
    return jnp.where(pick, slow, fast).astype(jnp.float32)


def set_ends(entries, key, smallest, top_value):
    longest = entries.shape.index(max(entries.shape))
    spots = []
    for shift in (0, 1):
        where = [jax.random.randint(jax.random.fold_in(key, axis), (), 0, length) for axis, length in enumerate(entries.shape)]
        where[longest] = (where[longest] + shift) % entries.shape[longest]
        spots.append(tuple(where))
    return entries.at[spots[0]].set(smallest).at[spots[1]].set(top_value)


def block_levels(own_key, extent, cuts, least, largest):
    factor_of = 1.0
    for dim, shards_of in cuts:
        draws = jax.random.uniform(jax.random.fold_in(jax.random.fold_in(own_key, 6), dim), (shards_of,), jnp.float32, least / len(cuts), largest / len(cuts))
        factor_of = factor_of * jnp.repeat(jnp.exp(draws), extent[dim] // shards_of).reshape((-1,) + (1,) * (len(extent) - 1 - dim))
    return factor_of


def gaussian(stream_key, shape, deviation, reach, held_as=jnp.bfloat16):
    values = jax.random.normal(stream_key, shape, jnp.float32) * deviation
    return jnp.minimum(jnp.maximum(values, -reach), reach).astype(held_as)


def setup_inputs(seed: int = 0, part: int = 0) -> dict:
    seeds = jax.random.split(jax.random.key(seed), 12)
    part_keys = jax.random.split(jax.random.fold_in(seeds[11], part), 12)
    demand = set_ends(jax.random.randint(part_keys[0], (S, TOTAL), 0, 21), jax.random.fold_in(part_keys[0], 1), 0, 20).astype(jnp.int32)
    lead_offset = set_ends(jax.random.randint(part_keys[1], (S, TOTAL), 0, LEAD), jax.random.fold_in(part_keys[1], 1), 0, LEAD - 1).astype(jnp.int32)
    review = set_ends((jax.random.randint(part_keys[2], (S, TOTAL), 0, 512) < 1).astype(jnp.int32), jax.random.fold_in(part_keys[2], 1), 0, 1)
    scenario_id = set_ends(jax.random.randint(part_keys[3], (S,), 0, NSCEN), jax.random.fold_in(part_keys[3], 1), 0, NSCEN - 1).astype(jnp.int32)
    initial_state = gaussian(part_keys[4], (S, H), 0.5, 2.5, jnp.float32)
    guess = jnp.clip(jax.random.uniform(part_keys[5], (S, TOTAL, H), jnp.float32, -0.9, 0.9) * block_levels(part_keys[5], (S, TOTAL, H), ((1, 16),), -0.4, 0.0), -0.9, 0.9)
    input_weight = gaussian(seeds[6], (2 * LEAD, 3 * H), (2 * LEAD) ** -0.5, 1.5, jnp.float32)
    scenario_table = gaussian(seeds[7], (NSCEN, 3 * H), 0.5, 3.0, jnp.float32)
    recur_weight = gaussian(seeds[8], (H, 3 * H), H ** -0.5, 0.5, jnp.float32)
    update_bias = draw_update_bias(jax.random.fold_in(seeds[11], 71), part)
    review_depth = jnp.clip(jax.random.uniform(seeds[10], (H,), jnp.float32, 0.8, 0.95), 0.8, 0.95)
    return {"demand": demand, "lead_offset": lead_offset, "review": review, "scenario_id": scenario_id, "initial_state": initial_state, "guess": guess, "input_weight": input_weight, "scenario_table": scenario_table, "recur_weight": recur_weight, "update_bias": update_bias, "review_depth": review_depth}


HIGH = lax.Precision.HIGHEST


def build_inputs(demand, lead_offset, review, scenario_id, input_weight, scenario_table, review_depth):
    lag_values = demand.astype(jnp.float32) * 0.125
    extended = jnp.concatenate([jnp.zeros((S, LEAD - 1), dtype=lag_values.dtype), lag_values], axis=1)
    lags = jnp.stack([extended[:, LEAD - 1 - j:LEAD - 1 - j + TOTAL] for j in range(LEAD)], axis=-1)
    onehot = (lead_offset[:, :, None] == jnp.arange(LEAD, dtype=jnp.int32)[None, None, :]).astype(lag_values.dtype)
    feats = jnp.concatenate([lags, onehot], axis=-1)
    xin = jnp.einsum("stf,fg->tsg", feats, input_weight, precision=HIGH)
    xin = xin + scenario_table[scenario_id][None, :, :]
    mult = 1.0 - review_depth[None, None, :] * jnp.transpose(review).astype(lag_values.dtype)[:, :, None]
    return xin, mult


def reference(demand, lead_offset, review, scenario_id, initial_state, guess, input_weight, scenario_table, recur_weight, update_bias, review_depth):
    xin, mult = build_inputs(demand, lead_offset, review, scenario_id, input_weight, scenario_table, review_depth)
    traj = jnp.transpose(guess, (1, 0, 2))

    def advance(state, inputs):
        prior, xrow, mrow = inputs
        recur = jnp.dot(prior, recur_weight, precision=HIGH)
        gate_z = jax.nn.sigmoid((xrow[:, :H] + recur[:, :H] + update_bias) * mrow)
        gate_r = jax.nn.sigmoid(xrow[:, H:2 * H] + recur[:, H:2 * H])
        cand = jnp.tanh(xrow[:, 2 * H:] + gate_r * recur[:, 2 * H:])
        fresh = (1.0 - gate_z) * cand + gate_z * prior
        delta = state - prior
        moved = jnp.dot(delta, recur_weight, precision=HIGH)
        coef_z = (prior - cand) * gate_z * (1.0 - gate_z) * mrow
        coef_n = (1.0 - gate_z) * (1.0 - cand * cand)
        product = gate_z * delta + coef_z * moved[:, :H] + coef_n * (gate_r * moved[:, 2 * H:] + recur[:, 2 * H:] * gate_r * (1.0 - gate_r) * moved[:, H:2 * H])
        following = fresh + product
        return following, following

    for turn in range(NEWTON):
        prior_seq = jnp.concatenate([initial_state[None], traj[:-1]], axis=0)
        final_state, traj = lax.scan(advance, initial_state, (prior_seq, xin, mult))
    return jnp.transpose(traj, (1, 0, 2))
```

```python
import functools

import jax
import jax.numpy as jnp
from jax import lax
from jax.experimental import pallas as pl
from jax.experimental.pallas import tpu as pltpu
from jax.sharding import PartitionSpec as P

LEAD = 8
NEWTON = 2
EXACT = (True, True)
MESH = pl.DeviceIdType.MESH
F32 = jnp.float32
BF16 = jnp.bfloat16


def split(value):
    high = value.astype(BF16)
    return high, (value - high.astype(F32)).astype(BF16)


def dot(a, b):
    return jnp.dot(a, b, preferred_element_type=F32)


def dot3(value, w_high, w_low):
    high, low = split(value)
    return dot(high, w_high) + dot(low, w_high) + dot(high, w_low)


def through(column, matrix):
    return jnp.sum(column * matrix, axis=0, keepdims=True)


def column_of(row):
    hidden = row.shape[1]
    return jnp.transpose(jnp.broadcast_to(row, (hidden, hidden)))


def kernel(
    sid_ref, demand_ref, lead_ref, review_ref, init_ref, guess_ref, iw_ref, table_ref, rw_ref, ub_ref, depth_ref,
    out_ref,
    sbuf, held, old, wh, wl, xin, mult, co_z, co_cz, co_n, co_r, err, pre, aff, dsend, dtake, traj,
    send_sem, rim_sem, recv_sem, rim_recv, chain_send, chain_recv, out_send, out_recv,
):
    scen, periods, hidden = guess_ref.shape
    inner = lax.axis_size("tm")
    links = lax.axis_size("slab") * inner // scen
    place = lax.axis_index("slab") * inner + lax.axis_index("tm")
    link = place // scen
    mine = lax.rem(place, scen)
    rows = scen * periods

    def device(at_link, member):
        index = at_link * scen + member
        return {"slab": index // inner, "tm": lax.rem(index, inner)}

    def peer(step):
        return lax.rem(mine + step, scen)

    first = link == 0
    final = link == links - 1
    tail = mine == scen - 1

    barrier = pltpu.get_barrier_semaphore()
    for step in range(1, scen):
        pl.semaphore_signal(barrier, inc=1, device_id=device(link, peer(step)), device_id_type=MESH)

    @pl.when(jnp.logical_not(first))
    def _():
        pl.semaphore_signal(barrier, inc=1, device_id=device(link - 1, mine), device_id_type=MESH)

    @pl.when(jnp.logical_not(first) & jnp.logical_not(tail))
    def _():
        pl.semaphore_signal(barrier, inc=1, device_id=device(link - 1, scen - 1), device_id_type=MESH)

    square = (periods, periods)
    diagonal = lax.broadcasted_iota(jnp.int32, square, 0) == lax.broadcasted_iota(jnp.int32, square, 1)
    lane = lax.broadcasted_iota(jnp.int32, (periods, hidden), 1)

    def upright(row):
        picked = jnp.where(diagonal, jnp.broadcast_to(row, square), 0.0)
        return jnp.broadcast_to(jnp.sum(picked, axis=1, keepdims=True), (periods, hidden))

    for s in range(scen):
        demand = upright(demand_ref[s : s + 1, :].astype(F32))
        lead = upright(lead_ref[s : s + 1, :].astype(F32))
        review = upright(review_ref[s : s + 1, :].astype(F32))
        sbuf[s, :, :hidden] = guess_ref[s]
        sbuf[s, :, hidden:] = jnp.where(lane < LEAD, demand, jnp.where(lane < 2 * LEAD, lead, review))

    pl.semaphore_wait(
        barrier,
        (scen - 1) + jnp.where(final, 0, 1) + jnp.where(jnp.logical_not(final) & tail, scen - 1, 0),
    )

    def exchange(step):
        to = peer(step)
        return pltpu.make_async_remote_copy(
            src_ref=sbuf.at[to],
            dst_ref=held.at[pl.ds(pl.multiple_of(8 + mine * periods, 8), periods)],
            send_sem=send_sem.at[step],
            recv_sem=recv_sem.at[scen - step],
            device_id=device(link, to),
            device_id_type=MESH,
        )

    def arrival(step):
        source = peer(step)
        return pltpu.make_async_remote_copy(
            src_ref=sbuf.at[0],
            dst_ref=held.at[pl.ds(pl.multiple_of(8 + source * periods, 8), periods)],
            send_sem=send_sem.at[step],
            recv_sem=recv_sem.at[step],
            device_id=device(link, source),
            device_id_type=MESH,
        )

    def rim(member):
        return pltpu.make_async_remote_copy(
            src_ref=sbuf.at[member, pl.ds(periods - 8, 8)],
            dst_ref=held.at[pl.ds(0, 8)],
            send_sem=rim_sem.at[member],
            recv_sem=rim_recv,
            device_id=device(link + 1, member),
            device_id_type=MESH,
        )

    for step in range(1, scen):
        exchange(step).start()

    @pl.when(tail & jnp.logical_not(final))
    def _():
        for member in range(scen):
            rim(member).start()

    held[pl.ds(pl.multiple_of(8 + mine * periods, 8), periods), :] = sbuf[mine]

    @pl.when(first)
    def _():
        held[0:8, :hidden] = jnp.broadcast_to(init_ref[pl.ds(mine, 1), :], (8, hidden))
        held[0:8, hidden:] = jnp.zeros((8, hidden), F32)

    weights = rw_ref[...]
    w_high, w_low = split(weights)
    wh[...] = w_high
    wl[...] = w_low
    iw_high, iw_rest = split(iw_ref[...])
    iw_low = iw_rest
    table_row = table_ref[pl.ds(sid_ref[mine], 1), :]

    for step in range(1, scen):
        arrival(step).wait_recv()

    @pl.when(jnp.logical_not(first))
    def _():
        rim(0).wait_recv()

    lanes = lax.broadcasted_iota(jnp.int32, (rows, hidden), 1)
    feat = jnp.where(
        (lanes >= LEAD) & (lanes < 2 * LEAD) & (held[8:, hidden:] == (lanes - LEAD).astype(F32)), 1.0, 0.0
    )
    for j in range(LEAD):
        feat = jnp.where(lanes == j, held[8 - j : 8 - j + rows, hidden:] * 0.125, feat)
    feat = feat[:, : 2 * LEAD].astype(BF16)
    xin[...] = dot(feat, iw_high) + dot(feat, iw_low) + table_row
    review = jnp.broadcast_to(held[8:, 2 * hidden - 1 :], (rows, hidden))
    mult[...] = 1.0 - depth_ref[...] * review
    old[...] = held[:, :hidden]

    eye = jnp.where(
        lax.broadcasted_iota(jnp.int32, (hidden, hidden), 0) == lax.broadcasted_iota(jnp.int32, (hidden, hidden), 1),
        1.0,
        0.0,
    )
    pad = 16

    for turn in range(NEWTON):
        prior = old[7 : 7 + rows, :]
        recur = dot3(prior, wh[...], wl[...])
        m = mult[...]
        z = jax.nn.sigmoid((xin[:, :hidden] + recur[:, :hidden] + ub_ref[...]) * m)
        r = jax.nn.sigmoid(xin[:, hidden : 2 * hidden] + recur[:, hidden : 2 * hidden])
        un = recur[:, 2 * hidden :]
        n = jnp.tanh(xin[:, 2 * hidden :] + r * un)
        stay = 1.0 - z
        cn = stay * (1.0 - n * n) * r
        co_z[...] = z
        co_cz[...] = (prior - n) * z * stay * m
        co_n[...] = cn
        co_r[...] = cn * un * (1.0 - r)
        err[...] = stay * n + z * prior - old[8:, :]

        for b in range(scen):
            at = slice(b * periods, b * periods + 1)
            pre[0, b * hidden : (b + 1) * hidden, :] = (
                co_z[at, :] * eye
                + co_cz[at, :] * rw_ref[:, :hidden]
                + co_n[at, :] * rw_ref[:, 2 * hidden :]
                + co_r[at, :] * rw_ref[:, hidden : 2 * hidden]
            )
            aff[0, b : b + 1, :] = err[at, :]
        aff[0, scen:, :] = jnp.zeros((pad - scen, hidden), F32)

        def compose(t, carry):
            x = jnp.concatenate([pre[t - 1], aff[t - 1]], axis=0)
            if EXACT[turn]:
                moved = dot3(x, wh[...], wl[...])
            else:
                moved = dot(x.astype(BF16), wh[...])
            for b in range(scen):
                at = pl.ds(b * periods + t, 1)
                own = slice(b * hidden, (b + 1) * hidden)
                pre[t, own, :] = (
                    co_z[at, :] * x[own]
                    + co_cz[at, :] * moved[own, :hidden]
                    + co_n[at, :] * moved[own, 2 * hidden :]
                    + co_r[at, :] * moved[own, hidden : 2 * hidden]
                )
                row = slice(scen * hidden + b, scen * hidden + b + 1)
                aff[t, b : b + 1, :] = (
                    co_z[at, :] * x[row]
                    + co_cz[at, :] * moved[row, :hidden]
                    + co_n[at, :] * moved[row, 2 * hidden :]
                    + co_r[at, :] * moved[row, hidden : 2 * hidden]
                    + err[at, :]
                )
            aff[t, scen:, :] = jnp.zeros((pad - scen, hidden), F32)
            return carry

        lax.fori_loop(1, periods, compose, 0)

        onward = pltpu.make_async_remote_copy(
            src_ref=dsend.at[turn],
            dst_ref=dtake.at[turn],
            send_sem=chain_send.at[turn],
            recv_sem=chain_recv.at[turn],
            device_id=device(link + 1, mine),
            device_id_type=MESH,
        )

        @pl.when(first)
        def _():
            dtake[turn] = jnp.zeros((8, hidden), F32)

        @pl.when(jnp.logical_not(first))
        def _():
            onward.wait_recv()

        enter = dtake[turn, 0:1, :]
        entering = enter
        columns = []
        for b in range(scen):
            column = column_of(entering)
            columns.append(column)
            entering = aff[periods - 1, b : b + 1, :] + through(
                column, pre[periods - 1, b * hidden : (b + 1) * hidden, :]
            )
        dsend[turn] = jnp.broadcast_to(entering, (8, hidden))

        @pl.when(jnp.logical_not(final))
        def _():
            onward.start()

        target = old if turn + 1 < NEWTON else traj
        shift = 8 if turn + 1 < NEWTON else 0
        if turn + 1 < NEWTON:
            old[0:8, :] = old[0:8, :] + jnp.broadcast_to(enter, (8, hidden))
        for b in range(scen):
            for t in range(periods):
                at = b * periods + t
                target[shift + at : shift + at + 1, :] = (
                    old[8 + at : 9 + at, :]
                    + aff[t, b : b + 1, :]
                    + through(columns[b], pre[t, b * hidden : (b + 1) * hidden, :])
                )

    def back(step):
        to = peer(step)
        return pltpu.make_async_remote_copy(
            src_ref=traj.at[pl.ds(pl.multiple_of(to * periods, 8), periods)],
            dst_ref=out_ref.at[mine],
            send_sem=out_send.at[step],
            recv_sem=out_recv.at[scen - step],
            device_id=device(link, to),
            device_id_type=MESH,
        )

    def returned(step):
        source = peer(step)
        return pltpu.make_async_remote_copy(
            src_ref=traj.at[pl.ds(0, periods)],
            dst_ref=out_ref.at[source],
            send_sem=out_send.at[step],
            recv_sem=out_recv.at[step],
            device_id=device(link, source),
            device_id_type=MESH,
        )

    for step in range(1, scen):
        back(step).start()
    out_ref[mine] = traj[pl.ds(pl.multiple_of(mine * periods, 8), periods), :]

    for step in range(1, scen):
        exchange(step).wait_send()

    @pl.when(tail & jnp.logical_not(final))
    def _():
        for member in range(scen):
            rim(member).wait_send()

    @pl.when(jnp.logical_not(final))
    def _():
        for turn in range(NEWTON):
            pltpu.make_async_remote_copy(
                src_ref=dsend.at[turn],
                dst_ref=dtake.at[turn],
                send_sem=chain_send.at[turn],
                recv_sem=chain_recv.at[turn],
                device_id=device(link + 1, mine),
                device_id_type=MESH,
            ).wait_send()

    for step in range(1, scen):
        back(step).wait_send()
        returned(step).wait_recv()


def on_device(
    demand, lead_offset, review, scenario_id, initial_state, guess,
    input_weight, scenario_table, recur_weight, update_bias, review_depth,
):
    scen, periods, hidden = guess.shape
    rows = scen * periods
    vmem = pl.BlockSpec(memory_space=pltpu.VMEM)
    dma = pltpu.SemaphoreType.DMA
    tile = pltpu.VMEM((rows, hidden), F32)
    return pl.pallas_call(
        kernel,
        out_shape=jax.ShapeDtypeStruct(guess.shape, F32),
        in_specs=[pl.BlockSpec(memory_space=pltpu.SMEM)] + [vmem] * 10,
        out_specs=vmem,
        scratch_shapes=[
            pltpu.VMEM((scen, periods, 2 * hidden), F32),
            pltpu.VMEM((8 + rows, 2 * hidden), F32),
            pltpu.VMEM((8 + rows, hidden), F32),
            pltpu.VMEM((hidden, 3 * hidden), BF16),
            pltpu.VMEM((hidden, 3 * hidden), BF16),
            pltpu.VMEM((rows, 3 * hidden), F32),
            tile, tile, tile, tile, tile, tile,
            pltpu.VMEM((periods, scen * hidden, hidden), F32),
            pltpu.VMEM((periods, 16, hidden), F32),
            pltpu.VMEM((NEWTON, 8, hidden), F32),
            pltpu.VMEM((NEWTON, 8, hidden), F32),
            tile,
            dma((scen,)), dma((scen,)), dma((scen,)), dma(()), dma((NEWTON,)), dma((NEWTON,)), dma((scen,)), dma((scen,)),
        ],
        compiler_params=pltpu.CompilerParams(
            collective_id=0, has_side_effects=True, vmem_limit_bytes=40 * 1024 * 1024
        ),
        name="newton",
    )(
        scenario_id, demand, lead_offset, review, initial_state, guess, input_weight, scenario_table,
        recur_weight, update_bias[None], review_depth[None],
    )


def solution(mesh):
    return jax.shard_map(
        on_device,
        mesh=mesh,
        in_specs=(
            P("groups", ("slab", "tm")),
            P("groups", ("slab", "tm")),
            P("groups", ("slab", "tm")),
            P("groups"),
            P("groups", None),
            P("groups", ("slab", "tm"), None),
            P(),
            P(),
            P(),
            P(),
            P(),
        ),
        out_specs=P("groups", ("slab", "tm"), None),
        check_vma=False,
    )
```

```python
import functools

import jax
import jax.numpy as jnp
from jax import lax
from jax.experimental import pallas as pl
from jax.experimental.pallas import tpu as pltpu
from jax.sharding import PartitionSpec as P

LEAD = 8
NEWTON = 2
EXACT = (False, False)
MESH = pl.DeviceIdType.MESH
F32 = jnp.float32
BF16 = jnp.bfloat16


def split(value):
    high = value.astype(BF16)
    return high, (value - high.astype(F32)).astype(BF16)


def dot(a, b):
    return jnp.dot(a, b, preferred_element_type=F32)


def dot3(value, w_high, w_low):
    high, low = split(value)
    return dot(jnp.concatenate([high, low], axis=1), jnp.concatenate([w_high, w_high], axis=0)) + dot(high, w_low)


def through(column, matrix):
    return jnp.sum(column * matrix, axis=0, keepdims=True)


def column_of(row):
    hidden = row.shape[1]
    return jnp.transpose(jnp.broadcast_to(row, (hidden, hidden)))


def kernel(
    sid_hbm, demand_hbm, lead_hbm, review_hbm, init_hbm, guess_hbm, iw_hbm, table_hbm, rw_hbm, ub_hbm, depth_hbm,
    out_ref,
    sid_ref, demand_ref, lead_ref, review_ref, init_ref, iw_ref, table_ref, rw_ref, ub_ref, depth_ref, in_sem,
    sbuf, held, old, wh, wl, xin, mult, co_z, co_cz, co_n, co_r, err, pre, aff, dsend, dtake, traj, reach, reach_row,
    send_sem, rim_sem, recv_sem, rim_recv, chain_send, chain_recv, out_send, out_recv,
):
    scen, periods, hidden = guess_hbm.shape
    loads = [
        pltpu.make_async_copy(source, target, in_sem.at[i])
        for i, (source, target) in enumerate(
            [
                (demand_hbm, demand_ref),
                (lead_hbm, lead_ref),
                (review_hbm, review_ref),
                (guess_hbm, sbuf.at[:, :, pl.ds(0, hidden)]),
                (rw_hbm, rw_ref),
                (init_hbm, init_ref),
                (iw_hbm, iw_ref),
                (table_hbm, table_ref),
                (ub_hbm, ub_ref),
                (depth_hbm, depth_ref),
                (sid_hbm, sid_ref),
            ]
        )
    ]
    for load in loads:
        load.start()
    inner = lax.axis_size("tm")
    links = lax.axis_size("slab") * inner // scen
    place = lax.axis_index("slab") * inner + lax.axis_index("tm")
    link = place // scen
    mine = lax.rem(place, scen)
    rows = scen * periods

    def device(at_link, member):
        index = at_link * scen + member
        return {"slab": index // inner, "tm": lax.rem(index, inner)}

    def peer(step):
        return lax.rem(mine + step, scen)

    first = link == 0
    final = link == links - 1
    tail = mine == scen - 1

    barrier = pltpu.get_barrier_semaphore()
    for step in range(1, scen):
        pl.semaphore_signal(barrier, inc=1, device_id=device(link, peer(step)), device_id_type=MESH)

    @pl.when(jnp.logical_not(first))
    def _():
        pl.semaphore_signal(barrier, inc=1, device_id=device(link - 1, mine), device_id_type=MESH)

    @pl.when(jnp.logical_not(first) & jnp.logical_not(tail))
    def _():
        pl.semaphore_signal(barrier, inc=1, device_id=device(link - 1, scen - 1), device_id_type=MESH)

    square = (periods, periods)
    diagonal = lax.broadcasted_iota(jnp.int32, square, 0) == lax.broadcasted_iota(jnp.int32, square, 1)
    lane = lax.broadcasted_iota(jnp.int32, (periods, hidden), 1)

    def upright(row):
        picked = jnp.where(diagonal, jnp.broadcast_to(row, square), 0.0)
        return jnp.broadcast_to(jnp.sum(picked, axis=1, keepdims=True), (periods, hidden))

    for load in loads[:4]:
        load.wait()
    for s in range(scen):
        demand = upright(demand_ref[s : s + 1, :].astype(F32))
        lead = upright(lead_ref[s : s + 1, :].astype(F32))
        review = upright(review_ref[s : s + 1, :].astype(F32))
        sbuf[s, :, hidden:] = jnp.where(lane < LEAD, demand, jnp.where(lane < 2 * LEAD, lead, review))

    pl.semaphore_wait(
        barrier,
        (scen - 1) + jnp.where(final, 0, 1) + jnp.where(jnp.logical_not(final) & tail, scen - 1, 0),
    )

    def exchange(step):
        to = peer(step)
        return pltpu.make_async_remote_copy(
            src_ref=sbuf.at[to],
            dst_ref=held.at[pl.ds(pl.multiple_of(8 + mine * periods, 8), periods)],
            send_sem=send_sem.at[step],
            recv_sem=recv_sem.at[scen - step],
            device_id=device(link, to),
            device_id_type=MESH,
        )

    def arrival(step):
        source = peer(step)
        return pltpu.make_async_remote_copy(
            src_ref=sbuf.at[0],
            dst_ref=held.at[pl.ds(pl.multiple_of(8 + source * periods, 8), periods)],
            send_sem=send_sem.at[step],
            recv_sem=recv_sem.at[step],
            device_id=device(link, source),
            device_id_type=MESH,
        )

    def rim(member):
        return pltpu.make_async_remote_copy(
            src_ref=sbuf.at[member, pl.ds(periods - 8, 8)],
            dst_ref=held.at[pl.ds(0, 8)],
            send_sem=rim_sem.at[member],
            recv_sem=rim_recv,
            device_id=device(link + 1, member),
            device_id_type=MESH,
        )

    for step in range(1, scen):
        exchange(step).start()

    @pl.when(tail & jnp.logical_not(final))
    def _():
        for member in range(scen):
            rim(member).start()

    for load in loads[4:]:
        load.wait()
    held[pl.ds(pl.multiple_of(8 + mine * periods, 8), periods), :] = sbuf[mine]

    @pl.when(first)
    def _():
        held[0:8, :hidden] = jnp.broadcast_to(init_ref[pl.ds(mine, 1), :], (8, hidden))
        held[0:8, hidden:] = jnp.zeros((8, hidden), F32)

    weights = rw_ref[...]
    w_high, w_low = split(weights)
    wh[...] = w_high
    wl[...] = w_low
    iw_high, iw_rest = split(iw_ref[...])
    iw_low = iw_rest
    table_row = table_ref[pl.ds(sid_ref[mine], 1), :]

    for step in range(1, scen):
        arrival(step).wait_recv()

    @pl.when(jnp.logical_not(first))
    def _():
        rim(0).wait_recv()

    lanes = lax.broadcasted_iota(jnp.int32, (rows, hidden), 1)
    feat = jnp.where(
        (lanes >= LEAD) & (lanes < 2 * LEAD) & (held[8:, hidden:] == (lanes - LEAD).astype(F32)), 1.0, 0.0
    )
    for j in range(LEAD):
        feat = jnp.where(lanes == j, held[8 - j : 8 - j + rows, hidden:] * 0.125, feat)
    feat = feat[:, : 2 * LEAD].astype(BF16)
    xin[...] = dot(feat, iw_high) + dot(feat, iw_low) + table_row
    review = jnp.broadcast_to(held[8:, 2 * hidden - 1 :], (rows, hidden))
    mult[...] = 1.0 - depth_ref[...] * review
    old[...] = held[:, :hidden]

    eye = jnp.where(
        lax.broadcasted_iota(jnp.int32, (hidden, hidden), 0) == lax.broadcasted_iota(jnp.int32, (hidden, hidden), 1),
        1.0,
        0.0,
    )
    for t in range(periods):
        aff[t] = jnp.zeros(aff.shape[1:], F32)

    for turn in range(NEWTON):
        prior = old[7 : 7 + rows, :]
        recur = dot3(prior, wh[...], wl[...])
        m = mult[...]
        z = jax.nn.sigmoid((xin[:, :hidden] + recur[:, :hidden] + ub_ref[...]) * m)
        r = jax.nn.sigmoid(xin[:, hidden : 2 * hidden] + recur[:, hidden : 2 * hidden])
        un = recur[:, 2 * hidden :]
        n = jnp.tanh(xin[:, 2 * hidden :] + r * un)
        stay = 1.0 - z
        cn = stay * (1.0 - n * n) * r
        co_z[...] = z
        co_cz[...] = (prior - n) * z * stay * m
        co_n[...] = cn
        co_r[...] = cn * un * (1.0 - r)
        err[...] = stay * n + z * prior - old[8:, :]

        for b in range(scen):
            at = slice(b * periods, b * periods + 1)
            pre[0, b * hidden : (b + 1) * hidden, :] = (
                co_z[at, :] * eye
                + co_cz[at, :] * rw_ref[:, :hidden]
                + co_n[at, :] * rw_ref[:, 2 * hidden :]
                + co_r[at, :] * rw_ref[:, hidden : 2 * hidden]
            )
            aff[0, b : b + 1, :] = err[at, :]
            if not EXACT[turn]:
                aff[0, scen + b : scen + b + 1, :] = err[at, :] - err[at, :].astype(BF16).astype(F32)

        w_both = jnp.concatenate([wh[...], wl[...]], axis=0)

        def compose(t, carry):
            x = jnp.concatenate([pre[t - 1], aff[t - 1]], axis=0)
            high = x.astype(BF16)
            moved = dot(jnp.concatenate([high, high], axis=1), w_both)
            if EXACT[turn]:
                moved += dot((x - high.astype(F32)).astype(BF16), wh[...])
            for b in range(scen):
                at = pl.ds(b * periods + t, 1)
                own = slice(b * hidden, (b + 1) * hidden)
                pre[t, own, :] = (
                    co_z[at, :] * x[own]
                    + co_cz[at, :] * moved[own, :hidden]
                    + co_n[at, :] * moved[own, 2 * hidden :]
                    + co_r[at, :] * moved[own, hidden : 2 * hidden]
                )
                row = slice(scen * hidden + b, scen * hidden + b + 1)
                rest = slice(scen * hidden + scen + b, scen * hidden + scen + b + 1)
                pushed = moved[row] if EXACT[turn] else moved[row] + moved[rest]
                value = (
                    co_z[at, :] * x[row]
                    + co_cz[at, :] * pushed[:, :hidden]
                    + co_n[at, :] * pushed[:, 2 * hidden :]
                    + co_r[at, :] * pushed[:, hidden : 2 * hidden]
                    + err[at, :]
                )
                aff[t, b : b + 1, :] = value
                if not EXACT[turn]:
                    aff[t, scen + b : scen + b + 1, :] = value - value.astype(BF16).astype(F32)
            return carry

        lax.fori_loop(1, periods, compose, 0)

        last = periods - 1
        for b in range(scen):
            own = slice(b * hidden, (b + 1) * hidden)
            row = jnp.broadcast_to(aff[last, b : b + 1, :], (8, hidden))
            if b == 0:
                reach[0], reach_row[0] = pre[last, own, :], row
            else:
                joined = dot3(
                    jnp.concatenate([reach[b - 1], reach_row[b - 1]], axis=0), *split(pre[last, own, :])
                )
                reach[b], reach_row[b] = joined[:hidden], joined[hidden:] + row

        onward = pltpu.make_async_remote_copy(
            src_ref=dsend.at[turn],
            dst_ref=dtake.at[turn],
            send_sem=chain_send.at[turn],
            recv_sem=chain_recv.at[turn],
            device_id=device(link + 1, mine),
            device_id_type=MESH,
        )

        @pl.when(first)
        def _():
            dtake[turn] = jnp.zeros((8, hidden), F32)

        @pl.when(jnp.logical_not(first))
        def _():
            onward.wait_recv()

        enter = dtake[turn, 0:1, :]
        column = column_of(enter)
        whole = reach_row[scen - 1, 0:1, :] + through(column, reach[scen - 1])
        dsend[turn] = jnp.broadcast_to(whole, (8, hidden))

        @pl.when(jnp.logical_not(final))
        def _():
            onward.start()

        columns = [column]
        for b in range(scen - 1):
            columns.append(column_of(reach_row[b, 0:1, :] + through(column, reach[b])))

        target = old if turn + 1 < NEWTON else traj
        shift = 8 if turn + 1 < NEWTON else 0
        if turn + 1 < NEWTON:
            old[0:8, :] = old[0:8, :] + jnp.broadcast_to(enter, (8, hidden))
        for b in range(scen):
            for t in range(periods):
                at = b * periods + t
                target[shift + at : shift + at + 1, :] = (
                    old[8 + at : 9 + at, :]
                    + aff[t, b : b + 1, :]
                    + through(columns[b], pre[t, b * hidden : (b + 1) * hidden, :])
                )

    def back(step):
        to = peer(step)
        return pltpu.make_async_remote_copy(
            src_ref=traj.at[pl.ds(pl.multiple_of(to * periods, 8), periods)],
            dst_ref=out_ref.at[mine],
            send_sem=out_send.at[step],
            recv_sem=out_recv.at[scen - step],
            device_id=device(link, to),
            device_id_type=MESH,
        )

    def returned(step):
        source = peer(step)
        return pltpu.make_async_remote_copy(
            src_ref=traj.at[pl.ds(0, periods)],
            dst_ref=out_ref.at[source],
            send_sem=out_send.at[step],
            recv_sem=out_recv.at[step],
            device_id=device(link, source),
            device_id_type=MESH,
        )

    for step in range(1, scen):
        back(step).start()
    out_ref[mine] = traj[pl.ds(pl.multiple_of(mine * periods, 8), periods), :]

    for step in range(1, scen):
        exchange(step).wait_send()

    @pl.when(tail & jnp.logical_not(final))
    def _():
        for member in range(scen):
            rim(member).wait_send()

    @pl.when(jnp.logical_not(final))
    def _():
        for turn in range(NEWTON):
            pltpu.make_async_remote_copy(
                src_ref=dsend.at[turn],
                dst_ref=dtake.at[turn],
                send_sem=chain_send.at[turn],
                recv_sem=chain_recv.at[turn],
                device_id=device(link + 1, mine),
                device_id_type=MESH,
            ).wait_send()

    for step in range(1, scen):
        back(step).wait_send()
        returned(step).wait_recv()


def on_device(
    demand, lead_offset, review, scenario_id, initial_state, guess,
    input_weight, scenario_table, recur_weight, update_bias, review_depth,
):
    scen, periods, hidden = guess.shape
    rows = scen * periods
    vmem = pl.BlockSpec(memory_space=pltpu.VMEM)
    hbm = pl.BlockSpec(memory_space=pltpu.HBM)
    operands = (
        scenario_id, demand, lead_offset, review, initial_state, guess, input_weight, scenario_table,
        recur_weight, update_bias[None], review_depth[None],
    )
    staged = [
        (pltpu.SMEM if i == 0 else pltpu.VMEM)(o.shape, o.dtype) for i, o in enumerate(operands) if i != 5
    ]
    dma = pltpu.SemaphoreType.DMA
    tile = pltpu.VMEM((rows, hidden), F32)
    return pl.pallas_call(
        kernel,
        out_shape=jax.ShapeDtypeStruct(guess.shape, F32),
        in_specs=[hbm] * 11,
        out_specs=vmem,
        scratch_shapes=staged + [
            dma((11,)),
            pltpu.VMEM((scen, periods, 2 * hidden), F32),
            pltpu.VMEM((8 + rows, 2 * hidden), F32),
            pltpu.VMEM((8 + rows, hidden), F32),
            pltpu.VMEM((hidden, 3 * hidden), BF16),
            pltpu.VMEM((hidden, 3 * hidden), BF16),
            pltpu.VMEM((rows, 3 * hidden), F32),
            tile, tile, tile, tile, tile, tile,
            pltpu.VMEM((periods, scen * hidden, hidden), F32),
            pltpu.VMEM((periods, 16, hidden), F32),
            pltpu.VMEM((NEWTON, 8, hidden), F32),
            pltpu.VMEM((NEWTON, 8, hidden), F32),
            tile,
            pltpu.VMEM((scen, hidden, hidden), F32),
            pltpu.VMEM((scen, 8, hidden), F32),
            dma((scen,)), dma((scen,)), dma((scen,)), dma(()), dma((NEWTON,)), dma((NEWTON,)), dma((scen,)), dma((scen,)),
        ],
        compiler_params=pltpu.CompilerParams(
            collective_id=0, has_side_effects=True, vmem_limit_bytes=60 * 1024 * 1024
        ),
        name="newton",
    )(*operands)


def solution(mesh):
    return jax.shard_map(
        on_device,
        mesh=mesh,
        in_specs=(
            P("groups", ("slab", "tm")),
            P("groups", ("slab", "tm")),
            P("groups", ("slab", "tm")),
            P("groups"),
            P("groups", None),
            P("groups", ("slab", "tm"), None),
            P(),
            P(),
            P(),
            P(),
            P(),
        ),
        out_specs=P("groups", ("slab", "tm"), None),
        check_vma=False,
    )
```

```python
import functools

import jax
import jax.numpy as jnp
from jax import lax
from jax.experimental import pallas as pl
from jax.experimental.pallas import tpu as pltpu
from jax.sharding import PartitionSpec as P

LEAD = 8
NEWTON = 2
EXACT = (False, False)
MESH = pl.DeviceIdType.MESH
F32 = jnp.float32
BF16 = jnp.bfloat16


def split(value):
    high = value.astype(BF16)
    return high, (value - high.astype(F32)).astype(BF16)


def dot(a, b):
    return jnp.dot(a, b, preferred_element_type=F32)


def dot3(value, w_high, w_low):
    high, low = split(value)
    return dot(jnp.concatenate([high, low], axis=1), jnp.concatenate([w_high, w_high], axis=0)) + dot(high, w_low)


def through(column, matrix):
    return jnp.sum(column * matrix, axis=0, keepdims=True)


def column_of(row):
    hidden = row.shape[1]
    return jnp.transpose(jnp.broadcast_to(row, (hidden, hidden)))


def kernel(
    sid_hbm, demand_hbm, lead_hbm, review_hbm, init_hbm, guess_hbm, iw_hbm, table_hbm, rw_hbm, ub_hbm, depth_hbm,
    out_ref,
    sid_ref, demand_ref, lead_ref, review_ref, init_ref, iw_ref, table_ref, rw_ref, ub_ref, depth_ref, in_sem,
    sbuf, held, old, wh, wl, xin, mult, co_z, co_cz, co_n, co_r, err, pre, aff, dsend, dtake, traj, reach, reach_row,
    send_sem, rim_sem, recv_sem, rim_recv, chain_send, chain_recv, out_send, out_recv,
):
    scen, periods, hidden = guess_hbm.shape
    loads = [
        pltpu.make_async_copy(source, target, in_sem.at[i])
        for i, (source, target) in enumerate(
            [
                (demand_hbm, demand_ref),
                (lead_hbm, lead_ref),
                (review_hbm, review_ref),
                (guess_hbm, sbuf.at[:, :, pl.ds(0, hidden)]),
                (rw_hbm, rw_ref),
                (init_hbm, init_ref),
                (iw_hbm, iw_ref),
                (table_hbm, table_ref),
                (ub_hbm, ub_ref),
                (depth_hbm, depth_ref),
                (sid_hbm, sid_ref),
            ]
        )
    ]
    for load in loads:
        load.start()
    inner = lax.axis_size("tm")
    links = lax.axis_size("slab") * inner // scen
    place = lax.axis_index("slab") * inner + lax.axis_index("tm")
    link = place // scen
    mine = lax.rem(place, scen)
    rows = scen * periods

    def device(at_link, member):
        index = at_link * scen + member
        return {"slab": index // inner, "tm": lax.rem(index, inner)}

    def peer(step):
        return lax.rem(mine + step, scen)

    first = link == 0
    final = link == links - 1
    tail = mine == scen - 1

    barrier = pltpu.get_barrier_semaphore()
    for step in range(1, scen):
        pl.semaphore_signal(barrier, inc=1, device_id=device(link, peer(step)), device_id_type=MESH)

    @pl.when(jnp.logical_not(first))
    def _():
        pl.semaphore_signal(barrier, inc=1, device_id=device(link - 1, mine), device_id_type=MESH)

    @pl.when(jnp.logical_not(first) & jnp.logical_not(tail))
    def _():
        pl.semaphore_signal(barrier, inc=1, device_id=device(link - 1, scen - 1), device_id_type=MESH)

    square = (periods, periods)
    diagonal = lax.broadcasted_iota(jnp.int32, square, 0) == lax.broadcasted_iota(jnp.int32, square, 1)
    lane = lax.broadcasted_iota(jnp.int32, (periods, hidden), 1)

    def upright(row):
        picked = jnp.where(diagonal, jnp.broadcast_to(row, square), 0.0)
        return jnp.broadcast_to(jnp.sum(picked, axis=1, keepdims=True), (periods, hidden))

    for load in loads[:4]:
        load.wait()
    for s in range(scen):
        demand = upright(demand_ref[s : s + 1, :].astype(F32))
        lead = upright(lead_ref[s : s + 1, :].astype(F32))
        review = upright(review_ref[s : s + 1, :].astype(F32))
        sbuf[s, :, hidden:] = jnp.where(lane < LEAD, demand, jnp.where(lane < 2 * LEAD, lead, review))

    pl.semaphore_wait(
        barrier,
        (scen - 1) + jnp.where(final, 0, 1) + jnp.where(jnp.logical_not(final) & tail, scen - 1, 0),
    )

    def exchange(step):
        to = peer(step)
        return pltpu.make_async_remote_copy(
            src_ref=sbuf.at[to],
            dst_ref=held.at[pl.ds(pl.multiple_of(8 + mine * periods, 8), periods)],
            send_sem=send_sem.at[step],
            recv_sem=recv_sem.at[scen - step],
            device_id=device(link, to),
            device_id_type=MESH,
        )

    def arrival(step):
        source = peer(step)
        return pltpu.make_async_remote_copy(
            src_ref=sbuf.at[0],
            dst_ref=held.at[pl.ds(pl.multiple_of(8 + source * periods, 8), periods)],
            send_sem=send_sem.at[step],
            recv_sem=recv_sem.at[step],
            device_id=device(link, source),
            device_id_type=MESH,
        )

    def rim(member):
        return pltpu.make_async_remote_copy(
            src_ref=sbuf.at[member, pl.ds(periods - 8, 8)],
            dst_ref=held.at[pl.ds(0, 8)],
            send_sem=rim_sem.at[member],
            recv_sem=rim_recv,
            device_id=device(link + 1, member),
            device_id_type=MESH,
        )

    for step in range(1, scen):
        exchange(step).start()

    @pl.when(tail & jnp.logical_not(final))
    def _():
        for member in range(scen):
            rim(member).start()

    for load in loads[4:]:
        load.wait()
    held[pl.ds(pl.multiple_of(8 + mine * periods, 8), periods), :] = sbuf[mine]

    @pl.when(first)
    def _():
        held[0:8, :hidden] = jnp.broadcast_to(init_ref[pl.ds(mine, 1), :], (8, hidden))
        held[0:8, hidden:] = jnp.zeros((8, hidden), F32)

    weights = rw_ref[...]
    w_high, w_low = split(weights)
    wh[...] = w_high
    wl[...] = w_low
    iw_high, iw_rest = split(iw_ref[...])
    iw_low = iw_rest
    table_row = table_ref[pl.ds(sid_ref[mine], 1), :]

    for step in range(1, scen):
        arrival(step).wait_recv()

    @pl.when(jnp.logical_not(first))
    def _():
        rim(0).wait_recv()

    lanes = lax.broadcasted_iota(jnp.int32, (rows, hidden), 1)
    feat = jnp.where(
        (lanes >= LEAD) & (lanes < 2 * LEAD) & (held[8:, hidden:] == (lanes - LEAD).astype(F32)), 1.0, 0.0
    )
    for j in range(LEAD):
        feat = jnp.where(lanes == j, held[8 - j : 8 - j + rows, hidden:] * 0.125, feat)
    feat = feat[:, : 2 * LEAD].astype(BF16)
    xin[...] = dot(feat, iw_high) + dot(feat, iw_low) + table_row
    review = jnp.broadcast_to(held[8:, 2 * hidden - 1 :], (rows, hidden))
    mult[...] = 1.0 - depth_ref[...] * review
    old[...] = held[:, :hidden]

    eye = jnp.where(
        lax.broadcasted_iota(jnp.int32, (hidden, hidden), 0) == lax.broadcasted_iota(jnp.int32, (hidden, hidden), 1),
        1.0,
        0.0,
    )
    for t in range(periods):
        aff[t] = jnp.zeros(aff.shape[1:], F32)

    for turn in range(NEWTON):
        prior = old[7 : 7 + rows, :]
        recur = dot3(prior, wh[...], wl[...])
        m = mult[...]
        z = jax.nn.sigmoid((xin[:, :hidden] + recur[:, :hidden] + ub_ref[...]) * m)
        r = jax.nn.sigmoid(xin[:, hidden : 2 * hidden] + recur[:, hidden : 2 * hidden])
        un = recur[:, 2 * hidden :]
        n = jnp.tanh(xin[:, 2 * hidden :] + r * un)
        stay = 1.0 - z
        cn = stay * (1.0 - n * n) * r
        co_z[...] = z
        co_cz[...] = (prior - n) * z * stay * m
        co_n[...] = cn
        co_r[...] = cn * un * (1.0 - r)
        err[...] = stay * n + z * prior - old[8:, :]

        for b in range(scen):
            at = slice(b * periods, b * periods + 1)
            pre[0, b * hidden : (b + 1) * hidden, :] = (
                co_z[at, :] * eye
                + co_cz[at, :] * rw_ref[:, :hidden]
                + co_n[at, :] * rw_ref[:, 2 * hidden :]
                + co_r[at, :] * rw_ref[:, hidden : 2 * hidden]
            )
            aff[0, b : b + 1, :] = err[at, :]
            if not EXACT[turn]:
                aff[0, scen + b : scen + b + 1, :] = err[at, :] - err[at, :].astype(BF16).astype(F32)

        w_both = jnp.concatenate([wh[...], wl[...]], axis=0)

        def compose(t, carry):
            x = jnp.concatenate([pre[t - 1], aff[t - 1]], axis=0)
            high = x.astype(BF16)
            moved = dot(jnp.concatenate([high, high], axis=1), w_both)
            if EXACT[turn]:
                moved += dot((x - high.astype(F32)).astype(BF16), wh[...])
            for b in range(scen):
                at = pl.ds(b * periods + t, 1)
                own = slice(b * hidden, (b + 1) * hidden)
                pre[t, own, :] = (
                    co_z[at, :] * x[own]
                    + co_cz[at, :] * moved[own, :hidden]
                    + co_n[at, :] * moved[own, 2 * hidden :]
                    + co_r[at, :] * moved[own, hidden : 2 * hidden]
                )
                row = slice(scen * hidden + b, scen * hidden + b + 1)
                rest = slice(scen * hidden + scen + b, scen * hidden + scen + b + 1)
                pushed = moved[row] if EXACT[turn] else moved[row] + moved[rest]
                value = (
                    co_z[at, :] * x[row]
                    + co_cz[at, :] * pushed[:, :hidden]
                    + co_n[at, :] * pushed[:, 2 * hidden :]
                    + co_r[at, :] * pushed[:, hidden : 2 * hidden]
                    + err[at, :]
                )
                aff[t, b : b + 1, :] = value
                if not EXACT[turn]:
                    aff[t, scen + b : scen + b + 1, :] = value - value.astype(BF16).astype(F32)
            return carry

        lax.fori_loop(1, periods, compose, 0, unroll=True)

        last = periods - 1
        for b in range(scen):
            own = slice(b * hidden, (b + 1) * hidden)
            row = jnp.broadcast_to(aff[last, b : b + 1, :], (8, hidden))
            if b == 0:
                reach[0], reach_row[0] = pre[last, own, :], row
            else:
                joined = dot3(
                    jnp.concatenate([reach[b - 1], reach_row[b - 1]], axis=0), *split(pre[last, own, :])
                )
                reach[b], reach_row[b] = joined[:hidden], joined[hidden:] + row

        onward = pltpu.make_async_remote_copy(
            src_ref=dsend.at[turn],
            dst_ref=dtake.at[turn],
            send_sem=chain_send.at[turn],
            recv_sem=chain_recv.at[turn],
            device_id=device(link + 1, mine),
            device_id_type=MESH,
        )

        @pl.when(first)
        def _():
            dtake[turn] = jnp.zeros((8, hidden), F32)

        @pl.when(jnp.logical_not(first))
        def _():
            onward.wait_recv()

        enter = dtake[turn, 0:1, :]
        column = column_of(enter)
        whole = reach_row[scen - 1, 0:1, :] + through(column, reach[scen - 1])
        dsend[turn] = jnp.broadcast_to(whole, (8, hidden))

        @pl.when(jnp.logical_not(final))
        def _():
            onward.start()

        columns = [column]
        for b in range(scen - 1):
            columns.append(column_of(reach_row[b, 0:1, :] + through(column, reach[b])))

        target = old if turn + 1 < NEWTON else traj
        shift = 8 if turn + 1 < NEWTON else 0
        if turn + 1 < NEWTON:
            old[0:8, :] = old[0:8, :] + jnp.broadcast_to(enter, (8, hidden))
        for b in range(scen):
            for t in range(periods):
                at = b * periods + t
                target[shift + at : shift + at + 1, :] = (
                    old[8 + at : 9 + at, :]
                    + aff[t, b : b + 1, :]
                    + through(columns[b], pre[t, b * hidden : (b + 1) * hidden, :])
                )

    def back(step):
        to = peer(step)
        return pltpu.make_async_remote_copy(
            src_ref=traj.at[pl.ds(pl.multiple_of(to * periods, 8), periods)],
            dst_ref=out_ref.at[mine],
            send_sem=out_send.at[step],
            recv_sem=out_recv.at[scen - step],
            device_id=device(link, to),
            device_id_type=MESH,
        )

    def returned(step):
        source = peer(step)
        return pltpu.make_async_remote_copy(
            src_ref=traj.at[pl.ds(0, periods)],
            dst_ref=out_ref.at[source],
            send_sem=out_send.at[step],
            recv_sem=out_recv.at[step],
            device_id=device(link, source),
            device_id_type=MESH,
        )

    for step in range(1, scen):
        back(step).start()
    out_ref[mine] = traj[pl.ds(pl.multiple_of(mine * periods, 8), periods), :]

    for step in range(1, scen):
        exchange(step).wait_send()

    @pl.when(tail & jnp.logical_not(final))
    def _():
        for member in range(scen):
            rim(member).wait_send()

    @pl.when(jnp.logical_not(final))
    def _():
        for turn in range(NEWTON):
            pltpu.make_async_remote_copy(
                src_ref=dsend.at[turn],
                dst_ref=dtake.at[turn],
                send_sem=chain_send.at[turn],
                recv_sem=chain_recv.at[turn],
                device_id=device(link + 1, mine),
                device_id_type=MESH,
            ).wait_send()

    for step in range(1, scen):
        back(step).wait_send()
        returned(step).wait_recv()


def on_device(
    demand, lead_offset, review, scenario_id, initial_state, guess,
    input_weight, scenario_table, recur_weight, update_bias, review_depth,
):
    scen, periods, hidden = guess.shape
    rows = scen * periods
    vmem = pl.BlockSpec(memory_space=pltpu.VMEM)
    hbm = pl.BlockSpec(memory_space=pltpu.HBM)
    operands = (
        scenario_id, demand, lead_offset, review, initial_state, guess, input_weight, scenario_table,
        recur_weight, update_bias[None], review_depth[None],
    )
    staged = [
        (pltpu.SMEM if i == 0 else pltpu.VMEM)(o.shape, o.dtype) for i, o in enumerate(operands) if i != 5
    ]
    dma = pltpu.SemaphoreType.DMA
    tile = pltpu.VMEM((rows, hidden), F32)
    return pl.pallas_call(
        kernel,
        out_shape=jax.ShapeDtypeStruct(guess.shape, F32),
        in_specs=[hbm] * 11,
        out_specs=vmem,
        scratch_shapes=staged + [
            dma((11,)),
            pltpu.VMEM((scen, periods, 2 * hidden), F32),
            pltpu.VMEM((8 + rows, 2 * hidden), F32),
            pltpu.VMEM((8 + rows, hidden), F32),
            pltpu.VMEM((hidden, 3 * hidden), BF16),
            pltpu.VMEM((hidden, 3 * hidden), BF16),
            pltpu.VMEM((rows, 3 * hidden), F32),
            tile, tile, tile, tile, tile, tile,
            pltpu.VMEM((periods, scen * hidden, hidden), F32),
            pltpu.VMEM((periods, 16, hidden), F32),
            pltpu.VMEM((NEWTON, 8, hidden), F32),
            pltpu.VMEM((NEWTON, 8, hidden), F32),
            tile,
            pltpu.VMEM((scen, hidden, hidden), F32),
            pltpu.VMEM((scen, 8, hidden), F32),
            dma((scen,)), dma((scen,)), dma((scen,)), dma(()), dma((NEWTON,)), dma((NEWTON,)), dma((scen,)), dma((scen,)),
        ],
        compiler_params=pltpu.CompilerParams(
            collective_id=0, has_side_effects=True, vmem_limit_bytes=60 * 1024 * 1024
        ),
        name="newton",
    )(*operands)


def solution(mesh):
    return jax.shard_map(
        on_device,
        mesh=mesh,
        in_specs=(
            P("groups", ("slab", "tm")),
            P("groups", ("slab", "tm")),
            P("groups", ("slab", "tm")),
            P("groups"),
            P("groups", None),
            P("groups", ("slab", "tm"), None),
            P(),
            P(),
            P(),
            P(),
            P(),
        ),
        out_specs=P("groups", ("slab", "tm"), None),
        check_vma=False,
    )
```

```python
import functools

import jax
import jax.numpy as jnp
from jax import lax
from jax.experimental import pallas as pl
from jax.experimental.pallas import tpu as pltpu
from jax.sharding import PartitionSpec as P

LEAD = 8
NEWTON = 2
EXACT = (False, False)
MESH = pl.DeviceIdType.MESH
F32 = jnp.float32
BF16 = jnp.bfloat16


def split(value):
    high = value.astype(BF16)
    return high, (value - high.astype(F32)).astype(BF16)


def dot(a, b):
    return jnp.dot(a, b, preferred_element_type=F32)


def dot3(value, w_high, w_low):
    high, low = split(value)
    return dot(jnp.concatenate([high, low], axis=1), jnp.concatenate([w_high, w_high], axis=0)) + dot(high, w_low)


def through(column, matrix):
    return jnp.sum(column * matrix, axis=0, keepdims=True)


def column_of(row):
    hidden = row.shape[1]
    return jnp.transpose(jnp.broadcast_to(row, (hidden, hidden)))


def kernel(
    sid_hbm, demand_hbm, lead_hbm, review_hbm, init_hbm, guess_hbm, iw_hbm, table_hbm, rw_hbm, ub_hbm, depth_hbm,
    out_ref,
    sid_ref, demand_ref, lead_ref, review_ref, init_ref, iw_ref, table_ref, rw_ref, ub_ref, depth_ref, in_sem,
    sbuf, held, old, wh, wl, xin, mult, co_z, co_cz, co_n, co_r, err, pre, aff, dsend, dtake, traj, reach, reach_row,
    send_sem, rim_sem, recv_sem, rim_recv, chain_send, chain_recv, out_send, out_recv,
):
    scen, periods, hidden = guess_hbm.shape
    loads = [
        pltpu.make_async_copy(source, target, in_sem.at[i])
        for i, (source, target) in enumerate(
            [
                (demand_hbm, demand_ref),
                (lead_hbm, lead_ref),
                (review_hbm, review_ref),
                (guess_hbm, sbuf.at[:, :, pl.ds(0, hidden)]),
                (rw_hbm, rw_ref),
                (init_hbm, init_ref),
                (iw_hbm, iw_ref),
                (table_hbm, table_ref),
                (ub_hbm, ub_ref),
                (depth_hbm, depth_ref),
                (sid_hbm, sid_ref),
            ]
        )
    ]
    inner = lax.axis_size("tm")
    links = lax.axis_size("slab") * inner // scen
    place = lax.axis_index("slab") * inner + lax.axis_index("tm")
    link = place // scen
    mine = lax.rem(place, scen)
    rows = scen * periods

    def device(at_link, member):
        index = at_link * scen + member
        return {"slab": index // inner, "tm": lax.rem(index, inner)}

    def peer(step):
        return lax.rem(mine + step, scen)

    first = link == 0
    final = link == links - 1
    tail = mine == scen - 1

    barrier = pltpu.get_barrier_semaphore()
    for step in range(1, scen):
        pl.semaphore_signal(barrier, inc=1, device_id=device(link, peer(step)), device_id_type=MESH)

    @pl.when(jnp.logical_not(first))
    def _():
        pl.semaphore_signal(barrier, inc=1, device_id=device(link - 1, mine), device_id_type=MESH)

    @pl.when(jnp.logical_not(first) & jnp.logical_not(tail))
    def _():
        pl.semaphore_signal(barrier, inc=1, device_id=device(link - 1, scen - 1), device_id_type=MESH)

    for load in loads:
        load.start()

    square = (periods, periods)
    diagonal = lax.broadcasted_iota(jnp.int32, square, 0) == lax.broadcasted_iota(jnp.int32, square, 1)
    lane = lax.broadcasted_iota(jnp.int32, (periods, hidden), 1)

    def upright(row):
        picked = jnp.where(diagonal, jnp.broadcast_to(row, square), 0.0)
        return jnp.broadcast_to(jnp.sum(picked, axis=1, keepdims=True), (periods, hidden))

    for load in loads[:4]:
        load.wait()
    for s in range(scen):
        demand = upright(demand_ref[s : s + 1, :].astype(F32))
        lead = upright(lead_ref[s : s + 1, :].astype(F32))
        review = upright(review_ref[s : s + 1, :].astype(F32))
        sbuf[s, :, hidden:] = jnp.where(lane < LEAD, demand, jnp.where(lane < 2 * LEAD, lead, review))

    pl.semaphore_wait(
        barrier,
        (scen - 1) + jnp.where(final, 0, 1) + jnp.where(jnp.logical_not(final) & tail, scen - 1, 0),
    )

    def exchange(step):
        to = peer(step)
        return pltpu.make_async_remote_copy(
            src_ref=sbuf.at[to],
            dst_ref=held.at[pl.ds(pl.multiple_of(8 + mine * periods, 8), periods)],
            send_sem=send_sem.at[step],
            recv_sem=recv_sem.at[scen - step],
            device_id=device(link, to),
            device_id_type=MESH,
        )

    def arrival(step):
        source = peer(step)
        return pltpu.make_async_remote_copy(
            src_ref=sbuf.at[0],
            dst_ref=held.at[pl.ds(pl.multiple_of(8 + source * periods, 8), periods)],
            send_sem=send_sem.at[step],
            recv_sem=recv_sem.at[step],
            device_id=device(link, source),
            device_id_type=MESH,
        )

    def rim(member):
        return pltpu.make_async_remote_copy(
            src_ref=sbuf.at[member, pl.ds(periods - 8, 8)],
            dst_ref=held.at[pl.ds(0, 8)],
            send_sem=rim_sem.at[member],
            recv_sem=rim_recv,
            device_id=device(link + 1, member),
            device_id_type=MESH,
        )

    for step in range(1, scen):
        exchange(step).start()

    @pl.when(tail & jnp.logical_not(final))
    def _():
        for member in range(scen):
            rim(member).start()

    for load in loads[4:]:
        load.wait()
    held[pl.ds(pl.multiple_of(8 + mine * periods, 8), periods), :] = sbuf[mine]

    @pl.when(first)
    def _():
        held[0:8, :hidden] = jnp.broadcast_to(init_ref[pl.ds(mine, 1), :], (8, hidden))
        held[0:8, hidden:] = jnp.zeros((8, hidden), F32)

    weights = rw_ref[...]
    w_high, w_low = split(weights)
    wh[...] = w_high
    wl[...] = w_low
    iw_high, iw_rest = split(iw_ref[...])
    iw_low = iw_rest
    table_row = table_ref[pl.ds(sid_ref[mine], 1), :]

    for step in range(1, scen):
        arrival(step).wait_recv()

    @pl.when(jnp.logical_not(first))
    def _():
        rim(0).wait_recv()

    lanes = lax.broadcasted_iota(jnp.int32, (rows, hidden), 1)
    feat = jnp.where(
        (lanes >= LEAD) & (lanes < 2 * LEAD) & (held[8:, hidden:] == (lanes - LEAD).astype(F32)), 1.0, 0.0
    )
    for j in range(LEAD):
        feat = jnp.where(lanes == j, held[8 - j : 8 - j + rows, hidden:] * 0.125, feat)
    feat = feat[:, : 2 * LEAD].astype(BF16)
    xin[...] = dot(feat, iw_high) + dot(feat, iw_low) + table_row
    review = jnp.broadcast_to(held[8:, 2 * hidden - 1 :], (rows, hidden))
    mult[...] = 1.0 - depth_ref[...] * review
    old[...] = held[:, :hidden]

    eye = jnp.where(
        lax.broadcasted_iota(jnp.int32, (hidden, hidden), 0) == lax.broadcasted_iota(jnp.int32, (hidden, hidden), 1),
        1.0,
        0.0,
    )
    for t in range(periods):
        aff[t] = jnp.zeros(aff.shape[1:], F32)

    def back(to):
        return pltpu.make_async_remote_copy(
            src_ref=traj.at[pl.ds(pl.multiple_of(to * periods, 8), periods)],
            dst_ref=out_ref.at[mine],
            send_sem=out_send.at[to],
            recv_sem=out_recv.at[mine],
            device_id=device(link, to),
            device_id_type=MESH,
        )

    for turn in range(NEWTON):
        prior = old[7 : 7 + rows, :]
        recur = dot3(prior, wh[...], wl[...])
        m = mult[...]
        z = jax.nn.sigmoid((xin[:, :hidden] + recur[:, :hidden] + ub_ref[...]) * m)
        r = jax.nn.sigmoid(xin[:, hidden : 2 * hidden] + recur[:, hidden : 2 * hidden])
        un = recur[:, 2 * hidden :]
        n = jnp.tanh(xin[:, 2 * hidden :] + r * un)
        stay = 1.0 - z
        cn = stay * (1.0 - n * n) * r
        co_z[...] = z
        co_cz[...] = (prior - n) * z * stay * m
        co_n[...] = cn
        co_r[...] = cn * un * (1.0 - r)
        err[...] = stay * n + z * prior - old[8:, :]

        for b in range(scen):
            at = slice(b * periods, b * periods + 1)
            pre[0, b * hidden : (b + 1) * hidden, :] = (
                co_z[at, :] * eye
                + co_cz[at, :] * rw_ref[:, :hidden]
                + co_n[at, :] * rw_ref[:, 2 * hidden :]
                + co_r[at, :] * rw_ref[:, hidden : 2 * hidden]
            )
            aff[0, b : b + 1, :] = err[at, :]
            if not EXACT[turn]:
                aff[0, scen + b : scen + b + 1, :] = err[at, :] - err[at, :].astype(BF16).astype(F32)

        w_both = jnp.concatenate([wh[...], wl[...]], axis=0)

        def compose(t, carry):
            x = jnp.concatenate([pre[t - 1], aff[t - 1]], axis=0)
            high = x.astype(BF16)
            moved = dot(jnp.concatenate([high, high], axis=1), w_both)
            if EXACT[turn]:
                moved += dot((x - high.astype(F32)).astype(BF16), wh[...])
            for b in range(scen):
                at = pl.ds(b * periods + t, 1)
                own = slice(b * hidden, (b + 1) * hidden)
                pre[t, own, :] = (
                    co_z[at, :] * x[own]
                    + co_cz[at, :] * moved[own, :hidden]
                    + co_n[at, :] * moved[own, 2 * hidden :]
                    + co_r[at, :] * moved[own, hidden : 2 * hidden]
                )
                row = slice(scen * hidden + b, scen * hidden + b + 1)
                rest = slice(scen * hidden + scen + b, scen * hidden + scen + b + 1)
                pushed = moved[row] if EXACT[turn] else moved[row] + moved[rest]
                value = (
                    co_z[at, :] * x[row]
                    + co_cz[at, :] * pushed[:, :hidden]
                    + co_n[at, :] * pushed[:, 2 * hidden :]
                    + co_r[at, :] * pushed[:, hidden : 2 * hidden]
                    + err[at, :]
                )
                aff[t, b : b + 1, :] = value
                if not EXACT[turn]:
                    aff[t, scen + b : scen + b + 1, :] = value - value.astype(BF16).astype(F32)
            return carry

        lax.fori_loop(1, periods, compose, 0, unroll=True)

        last = periods - 1
        for b in range(scen):
            own = slice(b * hidden, (b + 1) * hidden)
            row = jnp.broadcast_to(aff[last, b : b + 1, :], (8, hidden))
            if b == 0:
                reach[0], reach_row[0] = pre[last, own, :], row
            else:
                joined = dot3(
                    jnp.concatenate([reach[b - 1], reach_row[b - 1]], axis=0), *split(pre[last, own, :])
                )
                reach[b], reach_row[b] = joined[:hidden], joined[hidden:] + row

        onward = pltpu.make_async_remote_copy(
            src_ref=dsend.at[turn],
            dst_ref=dtake.at[turn],
            send_sem=chain_send.at[turn],
            recv_sem=chain_recv.at[turn],
            device_id=device(link + 1, mine),
            device_id_type=MESH,
        )

        @pl.when(first)
        def _():
            dtake[turn] = jnp.zeros((8, hidden), F32)

        @pl.when(jnp.logical_not(first))
        def _():
            onward.wait_recv()

        enter = dtake[turn, 0:1, :]
        column = column_of(enter)
        whole = reach_row[scen - 1, 0:1, :] + through(column, reach[scen - 1])
        dsend[turn] = jnp.broadcast_to(whole, (8, hidden))

        @pl.when(jnp.logical_not(final))
        def _():
            onward.start()

        columns = [column]
        for b in range(scen - 1):
            columns.append(column_of(reach_row[b, 0:1, :] + through(column, reach[b])))

        target = old if turn + 1 < NEWTON else traj
        shift = 8 if turn + 1 < NEWTON else 0
        if turn + 1 < NEWTON:
            old[0:8, :] = old[0:8, :] + jnp.broadcast_to(enter, (8, hidden))
        for b in range(scen):
            for t in range(periods):
                at = b * periods + t
                target[shift + at : shift + at + 1, :] = (
                    old[8 + at : 9 + at, :]
                    + aff[t, b : b + 1, :]
                    + through(columns[b], pre[t, b * hidden : (b + 1) * hidden, :])
                )
            if turn + 1 == NEWTON:

                @pl.when(mine != b)
                def _():
                    back(b).start()


    def returned(step):
        source = peer(step)
        return pltpu.make_async_remote_copy(
            src_ref=traj.at[pl.ds(0, periods)],
            dst_ref=out_ref.at[source],
            send_sem=out_send.at[source],
            recv_sem=out_recv.at[source],
            device_id=device(link, source),
            device_id_type=MESH,
        )

    out_ref[mine] = traj[pl.ds(pl.multiple_of(mine * periods, 8), periods), :]

    for step in range(1, scen):
        exchange(step).wait_send()

    @pl.when(tail & jnp.logical_not(final))
    def _():
        for member in range(scen):
            rim(member).wait_send()

    @pl.when(jnp.logical_not(final))
    def _():
        for turn in range(NEWTON):
            pltpu.make_async_remote_copy(
                src_ref=dsend.at[turn],
                dst_ref=dtake.at[turn],
                send_sem=chain_send.at[turn],
                recv_sem=chain_recv.at[turn],
                device_id=device(link + 1, mine),
                device_id_type=MESH,
            ).wait_send()

    for step in range(1, scen):
        back(peer(step)).wait_send()
        returned(step).wait_recv()


def on_device(
    demand, lead_offset, review, scenario_id, initial_state, guess,
    input_weight, scenario_table, recur_weight, update_bias, review_depth,
):
    scen, periods, hidden = guess.shape
    rows = scen * periods
    vmem = pl.BlockSpec(memory_space=pltpu.VMEM)
    hbm = pl.BlockSpec(memory_space=pltpu.HBM)
    operands = (
        scenario_id, demand, lead_offset, review, initial_state, guess, input_weight, scenario_table,
        recur_weight, update_bias[None], review_depth[None],
    )
    staged = [
        (pltpu.SMEM if i == 0 else pltpu.VMEM)(o.shape, o.dtype) for i, o in enumerate(operands) if i != 5
    ]
    dma = pltpu.SemaphoreType.DMA
    tile = pltpu.VMEM((rows, hidden), F32)
    return pl.pallas_call(
        kernel,
        out_shape=jax.ShapeDtypeStruct(guess.shape, F32),
        in_specs=[hbm] * 11,
        out_specs=vmem,
        scratch_shapes=staged + [
            dma((11,)),
            pltpu.VMEM((scen, periods, 2 * hidden), F32),
            pltpu.VMEM((8 + rows, 2 * hidden), F32),
            pltpu.VMEM((8 + rows, hidden), F32),
            pltpu.VMEM((hidden, 3 * hidden), BF16),
            pltpu.VMEM((hidden, 3 * hidden), BF16),
            pltpu.VMEM((rows, 3 * hidden), F32),
            tile, tile, tile, tile, tile, tile,
            pltpu.VMEM((periods, scen * hidden, hidden), F32),
            pltpu.VMEM((periods, 16, hidden), F32),
            pltpu.VMEM((NEWTON, 8, hidden), F32),
            pltpu.VMEM((NEWTON, 8, hidden), F32),
            tile,
            pltpu.VMEM((scen, hidden, hidden), F32),
            pltpu.VMEM((scen, 8, hidden), F32),
            dma((scen,)), dma((scen,)), dma((scen,)), dma(()), dma((NEWTON,)), dma((NEWTON,)), dma((scen,)), dma((scen,)),
        ],
        compiler_params=pltpu.CompilerParams(
            collective_id=0, has_side_effects=True, vmem_limit_bytes=60 * 1024 * 1024
        ),
        name="newton",
    )(*operands)


def solution(mesh):
    return jax.shard_map(
        on_device,
        mesh=mesh,
        in_specs=(
            P("groups", ("slab", "tm")),
            P("groups", ("slab", "tm")),
            P("groups", ("slab", "tm")),
            P("groups"),
            P("groups", None),
            P("groups", ("slab", "tm"), None),
            P(),
            P(),
            P(),
            P(),
            P(),
        ),
        out_specs=P("groups", ("slab", "tm"), None),
        check_vma=False,
    )
```

```python
import functools

import jax
import jax.numpy as jnp
from jax import lax
from jax.experimental import pallas as pl
from jax.experimental.pallas import tpu as pltpu
from jax.sharding import PartitionSpec as P

LEAD = 8
NEWTON = 2
EXACT = (False, False)
MESH = pl.DeviceIdType.MESH
F32 = jnp.float32
BF16 = jnp.bfloat16


def split(value):
    high = value.astype(BF16)
    return high, (value - high.astype(F32)).astype(BF16)


def dot(a, b):
    return jnp.dot(a, b, preferred_element_type=F32)


def dot3(value, w_high, w_low):
    high, low = split(value)
    return dot(jnp.concatenate([high, low], axis=1), jnp.concatenate([w_high, w_high], axis=0)) + dot(high, w_low)


def through(column, matrix):
    return jnp.sum(column * matrix, axis=0, keepdims=True)


def column_of(row):
    hidden = row.shape[1]
    return jnp.transpose(jnp.broadcast_to(row, (hidden, hidden)))


def kernel(
    sid_hbm, demand_hbm, lead_hbm, review_hbm, init_hbm, guess_hbm, iw_hbm, table_hbm, rw_hbm, ub_hbm, depth_hbm,
    out_ref,
    sid_ref, demand_ref, lead_ref, review_ref, init_ref, iw_ref, table_ref, rw_ref, ub_ref, depth_ref, in_sem,
    sbuf, held, old, wh, wl, xin, mult, co_z, co_cz, co_n, co_r, err, pre, aff, dsend, dtake, traj, reach, reach_row,
    send_sem, rim_sem, recv_sem, rim_recv, chain_send, chain_recv, out_send, out_recv,
):
    scen, periods, hidden = guess_hbm.shape
    loads = [
        pltpu.make_async_copy(source, target, in_sem.at[i])
        for i, (source, target) in enumerate(
            [
                (demand_hbm, demand_ref),
                (lead_hbm, lead_ref),
                (review_hbm, review_ref),
                (guess_hbm, sbuf.at[:, :, pl.ds(0, hidden)]),
                (rw_hbm, rw_ref),
                (init_hbm, init_ref),
                (iw_hbm, iw_ref),
                (table_hbm, table_ref),
                (ub_hbm, ub_ref),
                (depth_hbm, depth_ref),
                (sid_hbm, sid_ref),
            ]
        )
    ]
    inner = lax.axis_size("tm")
    links = lax.axis_size("slab") * inner // scen
    place = lax.axis_index("slab") * inner + lax.axis_index("tm")
    link = place // scen
    mine = lax.rem(place, scen)
    rows = scen * periods

    def device(at_link, member):
        index = at_link * scen + member
        return {"slab": index // inner, "tm": lax.rem(index, inner)}

    def peer(step):
        return lax.rem(mine + step, scen)

    first = link == 0
    final = link == links - 1
    tail = mine == scen - 1

    barrier = pltpu.get_barrier_semaphore()
    for step in range(1, scen):
        pl.semaphore_signal(barrier, inc=1, device_id=device(link, peer(step)), device_id_type=MESH)

    @pl.when(jnp.logical_not(first))
    def _():
        pl.semaphore_signal(barrier, inc=1, device_id=device(link - 1, mine), device_id_type=MESH)

    @pl.when(jnp.logical_not(first) & jnp.logical_not(tail))
    def _():
        pl.semaphore_signal(barrier, inc=1, device_id=device(link - 1, scen - 1), device_id_type=MESH)

    for load in loads:
        load.start()

    square = (periods, periods)
    diagonal = lax.broadcasted_iota(jnp.int32, square, 0) == lax.broadcasted_iota(jnp.int32, square, 1)
    lane = lax.broadcasted_iota(jnp.int32, (periods, hidden), 1)

    def upright(row):
        picked = jnp.where(diagonal, jnp.broadcast_to(row, square), 0.0)
        return jnp.broadcast_to(jnp.sum(picked, axis=1, keepdims=True), (periods, hidden))

    for load in loads[:4]:
        load.wait()
    for s in range(scen):
        demand = upright(demand_ref[s : s + 1, :].astype(F32))
        lead = upright(lead_ref[s : s + 1, :].astype(F32))
        review = upright(review_ref[s : s + 1, :].astype(F32))
        sbuf[s, :, hidden:] = jnp.where(lane < LEAD, demand, jnp.where(lane < 2 * LEAD, lead, review))

    pl.semaphore_wait(
        barrier,
        (scen - 1) + jnp.where(final, 0, 1) + jnp.where(jnp.logical_not(final) & tail, scen - 1, 0),
    )

    def exchange(step):
        to = peer(step)
        return pltpu.make_async_remote_copy(
            src_ref=sbuf.at[to],
            dst_ref=held.at[pl.ds(pl.multiple_of(8 + mine * periods, 8), periods)],
            send_sem=send_sem.at[step],
            recv_sem=recv_sem.at[scen - step],
            device_id=device(link, to),
            device_id_type=MESH,
        )

    def arrival(step):
        source = peer(step)
        return pltpu.make_async_remote_copy(
            src_ref=sbuf.at[0],
            dst_ref=held.at[pl.ds(pl.multiple_of(8 + source * periods, 8), periods)],
            send_sem=send_sem.at[step],
            recv_sem=recv_sem.at[step],
            device_id=device(link, source),
            device_id_type=MESH,
        )

    def rim(member):
        return pltpu.make_async_remote_copy(
            src_ref=sbuf.at[member, pl.ds(periods - 8, 8)],
            dst_ref=held.at[pl.ds(0, 8)],
            send_sem=rim_sem.at[member],
            recv_sem=rim_recv,
            device_id=device(link + 1, member),
            device_id_type=MESH,
        )

    @pl.when(tail & jnp.logical_not(final))
    def _():
        for member in range(scen):
            rim(member).start()

    for step in range(1, scen):
        exchange(step).start()

    for load in loads[4:]:
        load.wait()
    held[pl.ds(pl.multiple_of(8 + mine * periods, 8), periods), :] = sbuf[mine]

    @pl.when(first)
    def _():
        held[0:8, :hidden] = jnp.broadcast_to(init_ref[pl.ds(mine, 1), :], (8, hidden))
        held[0:8, hidden:] = jnp.zeros((8, hidden), F32)

    weights = rw_ref[...]
    w_high, w_low = split(weights)
    wh[...] = w_high
    wl[...] = w_low
    iw_high, iw_rest = split(iw_ref[...])
    iw_low = iw_rest
    table_row = table_ref[pl.ds(sid_ref[mine], 1), :]

    for step in range(1, scen):
        arrival(step).wait_recv()

    @pl.when(jnp.logical_not(first))
    def _():
        rim(0).wait_recv()

    lanes = lax.broadcasted_iota(jnp.int32, (rows, hidden), 1)
    feat = jnp.where(
        (lanes >= LEAD) & (lanes < 2 * LEAD) & (held[8:, hidden:] == (lanes - LEAD).astype(F32)), 1.0, 0.0
    )
    for j in range(LEAD):
        feat = jnp.where(lanes == j, held[8 - j : 8 - j + rows, hidden:] * 0.125, feat)
    feat = feat[:, : 2 * LEAD].astype(BF16)
    xin[...] = dot(feat, iw_high) + dot(feat, iw_low) + table_row
    review = jnp.broadcast_to(held[8:, 2 * hidden - 1 :], (rows, hidden))
    mult[...] = 1.0 - depth_ref[...] * review
    old[...] = held[:, :hidden]

    eye = jnp.where(
        lax.broadcasted_iota(jnp.int32, (hidden, hidden), 0) == lax.broadcasted_iota(jnp.int32, (hidden, hidden), 1),
        1.0,
        0.0,
    )
    for t in range(periods):
        aff[t] = jnp.zeros(aff.shape[1:], F32)

    def back(to):
        return pltpu.make_async_remote_copy(
            src_ref=traj.at[pl.ds(pl.multiple_of(to * periods, 8), periods)],
            dst_ref=out_ref.at[mine],
            send_sem=out_send.at[to],
            recv_sem=out_recv.at[mine],
            device_id=device(link, to),
            device_id_type=MESH,
        )

    for turn in range(NEWTON):
        prior = old[7 : 7 + rows, :]
        recur = dot3(prior, wh[...], wl[...])
        m = mult[...]
        z = jax.nn.sigmoid((xin[:, :hidden] + recur[:, :hidden] + ub_ref[...]) * m)
        r = jax.nn.sigmoid(xin[:, hidden : 2 * hidden] + recur[:, hidden : 2 * hidden])
        un = recur[:, 2 * hidden :]
        n = jnp.tanh(xin[:, 2 * hidden :] + r * un)
        stay = 1.0 - z
        cn = stay * (1.0 - n * n) * r
        co_z[...] = z
        co_cz[...] = (prior - n) * z * stay * m
        co_n[...] = cn
        co_r[...] = cn * un * (1.0 - r)
        err[...] = stay * n + z * prior - old[8:, :]

        for b in range(scen):
            at = slice(b * periods, b * periods + 1)
            pre[0, b * hidden : (b + 1) * hidden, :] = (
                co_z[at, :] * eye
                + co_cz[at, :] * rw_ref[:, :hidden]
                + co_n[at, :] * rw_ref[:, 2 * hidden :]
                + co_r[at, :] * rw_ref[:, hidden : 2 * hidden]
            )
            aff[0, b : b + 1, :] = err[at, :]
            if not EXACT[turn]:
                aff[0, scen + b : scen + b + 1, :] = err[at, :] - err[at, :].astype(BF16).astype(F32)

        w_both = jnp.concatenate([wh[...], wl[...]], axis=0)

        def compose(t, carry):
            x = jnp.concatenate([pre[t - 1], aff[t - 1]], axis=0)
            high = x.astype(BF16)
            moved = dot(jnp.concatenate([high, high], axis=1), w_both)
            if EXACT[turn]:
                moved += dot((x - high.astype(F32)).astype(BF16), wh[...])
            for b in range(scen):
                at = pl.ds(b * periods + t, 1)
                own = slice(b * hidden, (b + 1) * hidden)
                pre[t, own, :] = (
                    co_z[at, :] * x[own]
                    + co_cz[at, :] * moved[own, :hidden]
                    + co_n[at, :] * moved[own, 2 * hidden :]
                    + co_r[at, :] * moved[own, hidden : 2 * hidden]
                )
                row = slice(scen * hidden + b, scen * hidden + b + 1)
                rest = slice(scen * hidden + scen + b, scen * hidden + scen + b + 1)
                pushed = moved[row] if EXACT[turn] else moved[row] + moved[rest]
                value = (
                    co_z[at, :] * x[row]
                    + co_cz[at, :] * pushed[:, :hidden]
                    + co_n[at, :] * pushed[:, 2 * hidden :]
                    + co_r[at, :] * pushed[:, hidden : 2 * hidden]
                    + err[at, :]
                )
                aff[t, b : b + 1, :] = value
                if not EXACT[turn]:
                    aff[t, scen + b : scen + b + 1, :] = value - value.astype(BF16).astype(F32)
            return carry

        lax.fori_loop(1, periods, compose, 0, unroll=True)

        last = periods - 1
        for b in range(scen):
            own = slice(b * hidden, (b + 1) * hidden)
            row = jnp.broadcast_to(aff[last, b : b + 1, :], (8, hidden))
            if b == 0:
                reach[0], reach_row[0] = pre[last, own, :], row
            else:
                joined = dot3(
                    jnp.concatenate([reach[b - 1], reach_row[b - 1]], axis=0), *split(pre[last, own, :])
                )
                reach[b], reach_row[b] = joined[:hidden], joined[hidden:] + row

        onward = pltpu.make_async_remote_copy(
            src_ref=dsend.at[turn, pl.ds(0, 1)],
            dst_ref=dtake.at[turn, pl.ds(0, 1)],
            send_sem=chain_send.at[turn],
            recv_sem=chain_recv.at[turn],
            device_id=device(link + 1, mine),
            device_id_type=MESH,
        )

        @pl.when(first)
        def _():
            dtake[turn] = jnp.zeros((8, hidden), F32)

        @pl.when(jnp.logical_not(first))
        def _():
            onward.wait_recv()

        enter = dtake[turn, 0:1, :]
        column = column_of(enter)
        whole = reach_row[scen - 1, 0:1, :] + through(column, reach[scen - 1])
        dsend[turn] = jnp.broadcast_to(whole, (8, hidden))

        @pl.when(jnp.logical_not(final))
        def _():
            onward.start()

        columns = [column]
        for b in range(scen - 1):
            columns.append(column_of(reach_row[b, 0:1, :] + through(column, reach[b])))

        target = old if turn + 1 < NEWTON else traj
        shift = 8 if turn + 1 < NEWTON else 0
        if turn + 1 < NEWTON:
            old[0:8, :] = old[0:8, :] + jnp.broadcast_to(enter, (8, hidden))
        for b in range(scen):
            for t in range(periods):
                at = b * periods + t
                target[shift + at : shift + at + 1, :] = (
                    old[8 + at : 9 + at, :]
                    + aff[t, b : b + 1, :]
                    + through(columns[b], pre[t, b * hidden : (b + 1) * hidden, :])
                )
            if turn + 1 == NEWTON:

                @pl.when(mine != b)
                def _():
                    back(b).start()


    def returned(step):
        source = peer(step)
        return pltpu.make_async_remote_copy(
            src_ref=traj.at[pl.ds(0, periods)],
            dst_ref=out_ref.at[source],
            send_sem=out_send.at[source],
            recv_sem=out_recv.at[source],
            device_id=device(link, source),
            device_id_type=MESH,
        )

    out_ref[mine] = traj[pl.ds(pl.multiple_of(mine * periods, 8), periods), :]

    for step in range(1, scen):
        exchange(step).wait_send()

    @pl.when(tail & jnp.logical_not(final))
    def _():
        for member in range(scen):
            rim(member).wait_send()

    @pl.when(jnp.logical_not(final))
    def _():
        for turn in range(NEWTON):
            pltpu.make_async_remote_copy(
                src_ref=dsend.at[turn, pl.ds(0, 1)],
                dst_ref=dtake.at[turn, pl.ds(0, 1)],
                send_sem=chain_send.at[turn],
                recv_sem=chain_recv.at[turn],
                device_id=device(link + 1, mine),
                device_id_type=MESH,
            ).wait_send()

    for step in range(1, scen):
        back(peer(step)).wait_send()
        returned(step).wait_recv()


def on_device(
    demand, lead_offset, review, scenario_id, initial_state, guess,
    input_weight, scenario_table, recur_weight, update_bias, review_depth,
):
    scen, periods, hidden = guess.shape
    rows = scen * periods
    vmem = pl.BlockSpec(memory_space=pltpu.VMEM)
    hbm = pl.BlockSpec(memory_space=pltpu.HBM)
    operands = (
        scenario_id, demand, lead_offset, review, initial_state, guess, input_weight, scenario_table,
        recur_weight, update_bias[None], review_depth[None],
    )
    staged = [
        (pltpu.SMEM if i == 0 else pltpu.VMEM)(o.shape, o.dtype) for i, o in enumerate(operands) if i != 5
    ]
    dma = pltpu.SemaphoreType.DMA
    tile = pltpu.VMEM((rows, hidden), F32)
    return pl.pallas_call(
        kernel,
        out_shape=jax.ShapeDtypeStruct(guess.shape, F32),
        in_specs=[hbm] * 11,
        out_specs=vmem,
        scratch_shapes=staged + [
            dma((11,)),
            pltpu.VMEM((scen, periods, 2 * hidden), F32),
            pltpu.VMEM((8 + rows, 2 * hidden), F32),
            pltpu.VMEM((8 + rows, hidden), F32),
            pltpu.VMEM((hidden, 3 * hidden), BF16),
            pltpu.VMEM((hidden, 3 * hidden), BF16),
            pltpu.VMEM((rows, 3 * hidden), F32),
            tile, tile, tile, tile, tile, tile,
            pltpu.VMEM((periods, scen * hidden, hidden), F32),
            pltpu.VMEM((periods, 16, hidden), F32),
            pltpu.VMEM((NEWTON, 8, hidden), F32),
            pltpu.VMEM((NEWTON, 8, hidden), F32),
            tile,
            pltpu.VMEM((scen, hidden, hidden), F32),
            pltpu.VMEM((scen, 8, hidden), F32),
            dma((scen,)), dma((scen,)), dma((scen,)), dma(()), dma((NEWTON,)), dma((NEWTON,)), dma((scen,)), dma((scen,)),
        ],
        compiler_params=pltpu.CompilerParams(
            collective_id=0, has_side_effects=True, vmem_limit_bytes=60 * 1024 * 1024
        ),
        name="newton",
    )(*operands)


def solution(mesh):
    return jax.shard_map(
        on_device,
        mesh=mesh,
        in_specs=(
            P("groups", ("slab", "tm")),
            P("groups", ("slab", "tm")),
            P("groups", ("slab", "tm")),
            P("groups"),
            P("groups", None),
            P("groups", ("slab", "tm"), None),
            P(),
            P(),
            P(),
            P(),
            P(),
        ),
        out_specs=P("groups", ("slab", "tm"), None),
        check_vma=False,
    )
```
